32 devices in a mesh: wide: 8 (over z, x), narrow: 4 (over y, core).
Axes of the slice: x: 2, y: 2, z: 4, core: 2. Of those that a mesh axis runs over, the one named last changes fastest.
Arguments:
- spectra: bfloat16 [2, 32, 64, 32, 256], P(None, ('wide', 'narrow')), may hold values from -6 to 6
- out_grads: bfloat16 [2, 32, 64, 32, 256], P(None, ('wide', 'narrow')), may hold values from -0.75 to 0.75
- weights: float32 [2, 64, 32, 256, 256], P(None, 'wide', 'narrow'), may hold values from -6 to 6
- mode_factor: float32 [64, 8], replicated, may hold values from -2 to 2
- in_factor: float32 [256, 64], replicated, may hold values from -0.75 to 0.75
- out_factor: float32 [256, 64], replicated, may hold values from -0.75 to 0.75
- first_moment: float32 [2, 8, 32, 4096], P(None, None, 'narrow', 'wide'), may hold values from -60 to 60
- second_moment: float32 [8, 32, 4096], P(None, 'narrow', 'wide'), may hold values from 20 to 500
Outputs:
- new_weights: float32 [2, 64, 32, 256, 256], P(None, 'wide', 'narrow')
- new_first: float32 [2, 8, 32, 4096], P(None, None, 'narrow', 'wide')
- new_second: float32 [8, 32, 4096], P(None, 'narrow', 'wide')
The draws below stay inside these ranges and needn't reach their ends.
All inputs are finite; a program needn't handle non-finite values.
Results may differ from the reference program's by a relative error of at most 0.0003.
Values may be sent and summed in bfloat16 or wider, within the bound.
A program may use at most 192 MiB of HBM per device.

```python
import math
import jax
import jax.numpy as jnp
from jax import lax

KX = 64
KY = 32
C = 256
RX = 8
RI = 64
RO = 64
STEP = 1000
SAMPLES = 32


def block_scale(rng, extent, pieces, smallest, largest):
    loudness = 1.0
    for axis_at, blocks in pieces:
        heights = jax.random.uniform(jax.random.fold_in(jax.random.fold_in(rng, 6), axis_at), (blocks,), jnp.float32, smallest / len(pieces), largest / len(pieces))
        loudness = loudness * jnp.repeat(jnp.exp(heights), extent[axis_at] // blocks).reshape((-1,) + (1,) * (len(extent) - 1 - axis_at))
    return loudness


def gaussian(key, shape, deviation, reach, cuts=(), kind=jnp.bfloat16):
    entries = deviation * jax.random.normal(key, shape, jnp.float32)
    if cuts:
        entries = entries * block_scale(key, shape, cuts, -0.22, 0.18)
    return jnp.clip(entries, -reach, reach).astype(kind)


def setup_inputs(seed: int = 0) -> dict:
    arg_keys = jax.random.split(jax.random.key(seed), 9)
    return {
        "spectra": gaussian(arg_keys[0], (2, SAMPLES, KX, KY, C), 1.0, 6.0, ((1, 32),)),
        "out_grads": gaussian(arg_keys[1], (2, SAMPLES, KX, KY, C), (2 * SAMPLES) ** -0.5, 0.75, ((1, 32),)),
        "weights": gaussian(arg_keys[2], (2, KX, KY, C, C), 1.0, 6.0, ((1, 8), (2, 4)), jnp.float32),
        "mode_factor": gaussian(arg_keys[3], (KX, RX), RX ** -0.5, 2.0, (), jnp.float32),
        "in_factor": gaussian(arg_keys[4], (C, RI), RI ** -0.5, 0.75, (), jnp.float32),
        "out_factor": gaussian(arg_keys[5], (C, RO), RO ** -0.5, 0.75, (), jnp.float32),
        "first_moment": gaussian(arg_keys[6], (2, RX, KY, RI * RO), 10.0, 60.0, ((2, 4), (3, 8)), jnp.float32),
        "second_moment": jnp.clip(jnp.exp(math.log(500.0) - 3.218876 * jax.random.uniform(arg_keys[7], (RX, KY, RI * RO), jnp.float32) ** block_scale(arg_keys[7], (RX, KY, RI * RO), ((1, 4), (2, 8)), -0.2, 0.2)), 20.0, 500.0),
    }


highest = lax.Precision.HIGHEST

def reference(spectra, out_grads, weights, mode_factor, in_factor, out_factor, first_moment, second_moment):

    def project_row(operands):
        spectra_row, grads_row = operands
        products = jnp.einsum('pbmi,qbmo->pqmio', spectra_row.astype(jnp.float32), grads_row.astype(jnp.float32))
        grad = jnp.stack([products[0, 0] + products[1, 1], products[0, 1] - products[1, 0]])
        half_core = jnp.einsum('pmio,oc->pmic', grad, out_factor, precision=highest)
        return jnp.einsum('ia,pmic->pmac', in_factor, half_core, precision=highest)
    channel_core = lax.map(project_row, (jnp.moveaxis(spectra, 2, 0), jnp.moveaxis(out_grads, 2, 0)))
    core_grad = jnp.einsum('xr,xpmac->prmac', mode_factor, channel_core, precision=highest)
    core_grad = core_grad.reshape(2, RX, KY, RI * RO)
    new_first = 0.9 * first_moment + 0.1 * core_grad
    new_second = 0.999 * second_moment + 0.001 * (core_grad[0] * core_grad[0] + core_grad[1] * core_grad[1])
    first_scale = 1.0 / (1.0 - 0.9 ** STEP)
    second_scale = 1.0 / (1.0 - 0.999 ** STEP)
    core_step = new_first * first_scale / (jnp.sqrt(new_second * second_scale) + 1e-08)
    expanded = jnp.einsum('xr,prmk->xpmk', mode_factor, core_step, precision=highest)
    expanded = expanded.reshape(KX, 2, KY, RI, RO)

    def expand_row(operands):
        weight_row, expanded_row = operands
        left_part = jnp.einsum('pmac,oc->pmao', expanded_row, out_factor, precision=highest)
        change = jnp.einsum('ia,pmao->pmio', in_factor, left_part, precision=highest)
        return weight_row - 0.3 * change
    updated = lax.map(expand_row, (jnp.moveaxis(weights, 1, 0), expanded))
    new_weights = jnp.moveaxis(updated, 0, 1)
    return (new_weights, new_first, new_second)
```

```python
import functools

import jax
import jax.numpy as jnp
from jax import lax
from jax.experimental import pallas as pl
from jax.experimental.pallas import tpu as pltpu
from jax.sharding import PartitionSpec as P

STEP = 1000
MESH = pl.DeviceIdType.MESH
f32 = jnp.float32
bf16 = jnp.bfloat16


def split(value):
    high = value.astype(bf16)
    return high, (value - high.astype(f32)).astype(bf16)


def split_outside(value):
    high = lax.reduce_precision(value, 8, 7)
    low = lax.reduce_precision(value - high, 8, 7)
    return high.astype(bf16), low.astype(bf16)


def exchange_kernel(
    wide,
    narrow,
    groups,
    x_ref,
    g_ref,
    factor_ref,
    mode_ref,
    first_ref,
    second_ref,
    steps_ref,
    first_out,
    second_out,
    projected,
    sending,
    arrived,
    lhs_high,
    lhs_low,
    part,
    x_arrived,
    z_sending,
    z_arrived,
    exchange_sems,
    cross_sems,
    line_sems,
    gather_sems,
    forward_sems,
):
    lines = wide // 2
    w = lax.axis_index("wide")
    n = lax.axis_index("narrow")
    line = w // 2
    side = w % 2
    peer = line * 2 + (1 - side)
    ranks = mode_ref.shape[0]
    depth = arrived.shape[2]
    mine = arrived.shape[1]
    per = mine // groups
    rank_in = projected.shape[1] // 2
    share = rank_in // wide
    stride = sending.shape[0]

    def at_line(d):
        return ((line + d) % lines) * 2 + side

    def at_narrow(d):
        return (n + d) % narrow

    barrier = pltpu.get_barrier_semaphore()
    for d in range(1, narrow):
        pl.semaphore_signal(barrier, inc=1, device_id=(w, at_narrow(d)), device_id_type=MESH)
    for d in range(1, lines):
        pl.semaphore_signal(barrier, inc=1, device_id=(at_line(d), n), device_id_type=MESH)
    pl.semaphore_signal(barrier, inc=1, device_id=(peer, n), device_id_type=MESH)
    rows = 512

    def project(index, carry):
        at = pl.ds(pl.multiple_of(index * rows, rows), rows)
        xs, gs = x_ref[at, :], g_ref[at, :]
        total = jnp.dot(xs, factor_ref[0], preferred_element_type=f32)
        total += jnp.dot(gs, factor_ref[1], preferred_element_type=f32)
        total += jnp.dot(xs, factor_ref[2], preferred_element_type=f32)
        total += jnp.dot(gs, factor_ref[3], preferred_element_type=f32)
        projected[at, :] = total
        return carry

    lax.fori_loop(0, x_ref.shape[0] // rows, project, 0)

    def collect(ky):
        sending[ky] = projected[pl.ds(ky, depth, stride=stride), :]

    pl.semaphore_wait(barrier, narrow - 1 + lines - 1 + 1)
    exchanges = {}
    for group in range(groups):
        for d in list(range(1, narrow)) + [0]:
            start = at_narrow(d) * mine + group * per

            def one(index, carry):
                collect(start + index)
                return carry

            lax.fori_loop(0, per, one, 0)
            if d:
                copy = pltpu.make_async_remote_copy(
                    src_ref=sending.at[pl.ds(start, per)],
                    dst_ref=arrived.at[d - 1, pl.ds(group * per, per)],
                    send_sem=exchange_sems.at[0, group, d - 1],
                    recv_sem=exchange_sems.at[1, group, d - 1],
                    device_id=(w, at_narrow(d)),
                    device_id_type=MESH,
                )
                copy.start()
                exchanges[group, d] = copy

    half = depth // 2
    crossings, lined, gathers, forwards = {}, {}, {}, {}

    def multiply(ky, carry):
        lefts, rights = [], []
        for d in range(narrow):
            block = sending[n * mine + ky] if d == 0 else arrived[d - 1, ky]
            lefts.append(block.T[:rank_in])
            top, bottom = block[:half, rank_in:], block[half:, rank_in:]
            rights.append(jnp.concatenate([top, bottom], axis=1))
            rights.append(jnp.concatenate([bottom, -top], axis=1))
        left = jnp.concatenate(lefts, axis=1)
        right_high, right_low = split(jnp.concatenate(rights, axis=0))
        for r in range(ranks):
            high, low = split(left * mode_ref[r : r + 1, :])
            lhs_high[r * rank_in : (r + 1) * rank_in] = high
            lhs_low[r * rank_in : (r + 1) * rank_in] = low
        both = jnp.concatenate([right_high, right_low], axis=1)
        width = right_high.shape[1]
        wider = jnp.dot(lhs_high[...], both, preferred_element_type=f32)
        total = jnp.dot(lhs_low[...], right_high, preferred_element_type=f32)
        total += wider[:, :width] + wider[:, width:]
        for r in range(ranks):
            for owner in range(wide):
                at = r * rank_in + owner * share
                part[owner // 2, owner % 2, ky, r * share : (r + 1) * share] = total[at : at + share]
        return carry

    def stage_multiply(group):
        for d in range(1, narrow):
            exchanges[group, d].wait_recv()
        lax.fori_loop(group * per, (group + 1) * per, multiply, 0)
        for l in range(lines):
            copy = pltpu.make_async_remote_copy(
                src_ref=part.at[l, 1 - side, pl.ds(group * per, per)],
                dst_ref=x_arrived.at[l, pl.ds(group * per, per)],
                send_sem=cross_sems.at[0, group, l],
                recv_sem=cross_sems.at[1, group, l],
                device_id=(peer, n),
                device_id_type=MESH,
            )
            copy.start()
            crossings[group, l] = copy

    def stage_cross(group):
        at = pl.ds(group * per, per)
        for l in range(lines):
            crossings[group, l].wait_recv()
        for d in list(range(1, lines)) + [0]:
            to = (line + d) % lines
            z_sending[d, at] = x_arrived[to, at] + part[to, side, at]
            if d:
                copy = pltpu.make_async_remote_copy(
                    src_ref=z_sending.at[d, at],
                    dst_ref=z_arrived.at[d - 1, at],
                    send_sem=line_sems.at[0, group, d - 1],
                    recv_sem=line_sems.at[1, group, d - 1],
                    device_id=(at_line(d), n),
                    device_id_type=MESH,
                )
                copy.start()
                lined[group, d] = copy

    first_scale = 1.0 / (1.0 - 0.9**STEP)
    second_scale = 1.0 / (1.0 - 0.999**STEP)

    def send_steps(owner, group, device, send_sem, recv_sem):
        block = steps_ref.at[owner, pl.ds(group * per, per)]
        copy = pltpu.make_async_remote_copy(
            src_ref=block,
            dst_ref=block,
            send_sem=send_sem,
            recv_sem=recv_sem,
            device_id=(device, n),
            device_id_type=MESH,
        )
        copy.start()
        return copy

    def stage_adam(group):
        at = pl.ds(group * per, per)
        grad = z_sending[0, at]
        for d in range(1, lines):
            lined[group, d].wait_recv()
            grad += z_arrived[d - 1, at]
        new_first = 0.9 * first_ref[at] + 0.1 * grad
        square = grad * grad
        flat = square.reshape(-1, square.shape[-1])
        other = pltpu.roll(flat, flat.shape[-1] // 2, 1).reshape(square.shape)
        new_second = 0.999 * second_ref[at] + 0.001 * (square + other)
        first_out[at] = new_first
        second_out[at] = new_second
        steps_ref[w, at] = new_first * first_scale / (jnp.sqrt(new_second * second_scale) + 1e-08)
        forwards[group, 0] = send_steps(
            w, group, peer, forward_sems.at[0, group, 0], forward_sems.at[1, group, 0]
        )
        for d in range(1, lines):
            gathers[group, d] = send_steps(
                w, group, at_line(d), gather_sems.at[0, group, d - 1], gather_sems.at[1, group, d - 1]
            )

    def stage_forward(group):
        for d in range(1, lines):
            gathers[group, d].wait_recv()
            forwards[group, d] = send_steps(
                at_line(lines - d), group, peer, forward_sems.at[0, group, d], forward_sems.at[1, group, d]
            )

    for tick in range(groups + 3):
        for late, stage in enumerate((stage_multiply, stage_cross, stage_adam, stage_forward)):
            if 0 <= tick - late < groups:
                stage(tick - late)
    for copy in forwards.values():
        copy.wait_recv()
    for copies in (exchanges, crossings, lined, gathers, forwards):
        for copy in copies.values():
            copy.wait_send()


def update_kernel(mode_ref, steps_ref, weights_ref, out_ref_factor, in_ref_factor, result_ref):
    ky, tile = pl.program_id(0), pl.program_id(1)
    rows = weights_ref.shape[1]
    ranks = steps_ref.shape[1]
    rank_in = steps_ref.shape[2]
    width = steps_ref.shape[3]
    columns = weights_ref.shape[4]
    expanded = []
    for x in range(rows):
        total = mode_ref[tile * rows + x, 0] * steps_ref[0, 0]
        for r in range(1, ranks):
            total += mode_ref[tile * rows + x, r] * steps_ref[0, r]
        expanded.append(total)
    high, low = split(jnp.concatenate(expanded, axis=0))
    left = jnp.dot(high, out_ref_factor[0], preferred_element_type=f32)
    left += jnp.dot(low, out_ref_factor[0], preferred_element_type=f32)
    left += jnp.dot(high, out_ref_factor[1], preferred_element_type=f32)
    for x in range(rows):
        for p in range(2):
            high, low = split(left[x * rank_in : (x + 1) * rank_in, p * columns : (p + 1) * columns])
            change = jnp.dot(
                in_ref_factor[...],
                jnp.concatenate([high, low, high], axis=0),
                preferred_element_type=f32,
            )
            result_ref[p, x, 0] = weights_ref[p, x, 0] - change


def local(
    spectra, out_grads, weights, mode_factor, in_factor, out_factor, first_moment, second_moment
):
    wide = lax.axis_size("wide")
    narrow = lax.axis_size("narrow")
    samples = spectra.shape[1]
    assert samples == 1
    modes_first, modes_second, channels = spectra.shape[2:]
    first_mine = modes_first // wide
    second_mine = modes_second // narrow
    rank_in = in_factor.shape[1]
    rank_out = out_factor.shape[1]
    ranks = mode_factor.shape[1]
    share = rank_in // wide
    width = 2 * rank_out
    depth = 2 * modes_first
    lines = wide // 2
    groups = 4
    shard_rows = ranks * share

    in_high, in_low = split_outside(in_factor)
    out_high, out_low = split_outside(out_factor)
    none = jnp.zeros_like(in_high)
    factors = jnp.stack(
        [
            jnp.concatenate(pair, axis=1)
            for pair in ((in_high, none), (none, out_high), (in_low, none), (none, out_low))
        ]
    )
    modes = jnp.tile(mode_factor.T, (1, 2 * narrow))

    first = first_moment.reshape(2, ranks, second_mine, share, rank_out)
    first = first.transpose(2, 1, 3, 0, 4).reshape(second_mine, shard_rows, width)
    second = second_moment.reshape(ranks, second_mine, share, 1, rank_out)
    second = jnp.broadcast_to(second, (ranks, second_mine, share, 2, rank_out))
    second = second.transpose(1, 0, 2, 3, 4).reshape(second_mine, shard_rows, width)

    vmem = pl.BlockSpec(memory_space=pltpu.VMEM)
    steps, new_first, new_second = pl.pallas_call(
        functools.partial(exchange_kernel, wide, narrow, groups),
        out_shape=(
            jax.ShapeDtypeStruct((wide, second_mine, shard_rows, width), f32),
            jax.ShapeDtypeStruct((second_mine, shard_rows, width), f32),
            jax.ShapeDtypeStruct((second_mine, shard_rows, width), f32),
        ),
        in_specs=[vmem] * 6,
        out_specs=(vmem,) * 3,
        scratch_shapes=[
            pltpu.VMEM((depth * modes_second, width), f32),
            pltpu.VMEM((modes_second, depth, width), f32),
            pltpu.VMEM((narrow - 1, second_mine, depth, width), f32),
            pltpu.VMEM((ranks * rank_in, narrow * depth), bf16),
            pltpu.VMEM((ranks * rank_in, narrow * depth), bf16),
            pltpu.VMEM((lines, 2, second_mine, shard_rows, width), f32),
            pltpu.VMEM((lines, second_mine, shard_rows, width), f32),
            pltpu.VMEM((lines, second_mine, shard_rows, width), f32),
            pltpu.VMEM((lines - 1, second_mine, shard_rows, width), f32),
            pltpu.SemaphoreType.DMA((2, groups, narrow - 1)),
            pltpu.SemaphoreType.DMA((2, groups, lines)),
            pltpu.SemaphoreType.DMA((2, groups, lines - 1)),
            pltpu.SemaphoreType.DMA((2, groups, lines - 1)),
            pltpu.SemaphoreType.DMA((2, groups, lines)),
        ],
        compiler_params=pltpu.CompilerParams(
            collective_id=0, has_side_effects=True, vmem_limit_bytes=48 * 1024 * 1024
        ),
        name="core_exchange",
    )(
        spectra.reshape(depth * modes_second, channels),
        out_grads.reshape(depth * modes_second, channels),
        factors,
        modes,
        first,
        second,
    )

    steps = steps.reshape(wide, second_mine, ranks, share, width)
    steps = steps.transpose(1, 2, 0, 3, 4).reshape(second_mine, ranks, rank_in, width)

    rows = min(4, first_mine)
    clear = jnp.zeros((rank_out, channels), bf16)

    def both_parts(factor):
        flat = factor.T
        return jnp.concatenate(
            [jnp.concatenate([flat, clear], axis=1), jnp.concatenate([clear, flat], axis=1)], axis=0
        )

    out_pair = jnp.stack([both_parts(out_high), both_parts(out_low)])
    scaled_high, scaled_low = split_outside(0.3 * in_factor)
    in_stack = jnp.concatenate([scaled_high, scaled_high, scaled_low], axis=1)
    mine_rows = lax.dynamic_slice_in_dim(
        mode_factor, lax.axis_index("wide") * first_mine, first_mine, 0
    )
    block = pl.BlockSpec(
        (2, rows, 1, channels, channels), lambda ky, tile: (0, tile, ky, 0, 0)
    )
    new_weights = pl.pallas_call(
        update_kernel,
        grid=(second_mine, first_mine // rows),
        out_shape=jax.ShapeDtypeStruct(weights.shape, f32),
        in_specs=[
            pl.BlockSpec(memory_space=pltpu.SMEM),
            pl.BlockSpec((1, ranks, rank_in, width), lambda ky, tile: (ky, 0, 0, 0)),
            block,
            pl.BlockSpec(out_pair.shape, lambda ky, tile: (0, 0, 0)),
            pl.BlockSpec(in_stack.shape, lambda ky, tile: (0, 0)),
        ],
        out_specs=block,
        compiler_params=pltpu.CompilerParams(vmem_limit_bytes=48 * 1024 * 1024),
        name="weight_update",
    )(mine_rows, steps, weights, out_pair, in_stack)

    new_first = new_first.reshape(second_mine, ranks, share, 2, rank_out)
    new_first = new_first.transpose(3, 1, 0, 2, 4).reshape(first_moment.shape)
    new_second = new_second[:, :, :rank_out].reshape(second_mine, ranks, share, rank_out)
    new_second = new_second.transpose(1, 0, 2, 3).reshape(second_moment.shape)
    return (new_weights, new_first, new_second)


def solution(mesh):
    placed = (
        P(None, ("wide", "narrow"), None, None, None),
        P(None, ("wide", "narrow"), None, None, None),
        P(None, "wide", "narrow", None, None),
        P(),
        P(),
        P(),
        P(None, None, "narrow", "wide"),
        P(None, "narrow", "wide"),
    )
    return jax.shard_map(
        local,
        mesh=mesh,
        in_specs=placed,
        out_specs=(
            P(None, "wide", "narrow", None, None),
            P(None, None, "narrow", "wide"),
            P(None, "narrow", "wide"),
        ),
        check_vma=False,
    )
```

```python
import functools

import jax
import jax.numpy as jnp
from jax import lax
from jax.experimental import pallas as pl
from jax.experimental.pallas import tpu as pltpu
from jax.sharding import PartitionSpec as P

STEP = 1000
MESH = pl.DeviceIdType.MESH
f32 = jnp.float32
bf16 = jnp.bfloat16


def split(value):
    high = value.astype(bf16)
    return high, (value - high.astype(f32)).astype(bf16)


def exchange_kernel(
    wide,
    narrow,
    groups,
    x_ref,
    g_ref,
    in_ref,
    out_ref,
    mode_ref,
    first_ref,
    second_ref,
    steps_ref,
    first_out,
    second_out,
    projected,
    sending,
    arrived,
    lhs_high,
    lhs_low,
    part,
    x_arrived,
    z_sending,
    z_arrived,
    exchange_sems,
    cross_sems,
    line_sems,
    gather_sems,
    forward_sems,
):
    lines = wide // 2
    w = lax.axis_index("wide")
    n = lax.axis_index("narrow")
    line = w // 2
    side = w % 2
    peer = line * 2 + (1 - side)
    ranks = mode_ref.shape[0]
    depth = arrived.shape[2]
    mine = arrived.shape[1]
    per = mine // groups
    rank_in = projected.shape[1] // 2
    share = rank_in // wide
    stride = sending.shape[0]

    def at_line(d):
        return ((line + d) % lines) * 2 + side

    def at_narrow(d):
        return (n + d) % narrow

    barrier = pltpu.get_barrier_semaphore()
    for d in range(1, narrow):
        pl.semaphore_signal(barrier, inc=1, device_id=(w, at_narrow(d)), device_id_type=MESH)
    for d in range(1, lines):
        pl.semaphore_signal(barrier, inc=1, device_id=(at_line(d), n), device_id_type=MESH)
    pl.semaphore_signal(barrier, inc=1, device_id=(peer, n), device_id_type=MESH)
    rows = 512
    modes = jnp.concatenate([mode_ref[...]] * (2 * narrow), axis=1)
    none = jnp.zeros(in_ref.shape, f32)
    x_high, x_low = split(jnp.concatenate([in_ref[...], none], axis=0).T)
    g_high, g_low = split(jnp.concatenate([none, out_ref[...]], axis=0).T)

    def project(index, carry):
        at = pl.ds(pl.multiple_of(index * rows, rows), rows)
        xs, gs = x_ref[at, :], g_ref[at, :]
        total = jnp.dot(xs, x_high, preferred_element_type=f32)
        total += jnp.dot(gs, g_high, preferred_element_type=f32)
        total += jnp.dot(xs, x_low, preferred_element_type=f32)
        total += jnp.dot(gs, g_low, preferred_element_type=f32)
        projected[at, :] = total
        return carry

    lax.fori_loop(0, x_ref.shape[0] // rows, project, 0)

    def collect(ky):
        sending[ky] = projected[pl.ds(ky, depth, stride=stride), :]

    pl.semaphore_wait(barrier, narrow - 1 + lines - 1 + 1)
    exchanges = {}
    for group in range(groups):
        for d in list(range(1, narrow)) + [0]:
            start = at_narrow(d) * mine + group * per

            def one(index, carry):
                collect(start + index)
                return carry

            lax.fori_loop(0, per, one, 0)
            if d:
                copy = pltpu.make_async_remote_copy(
                    src_ref=sending.at[pl.ds(start, per)],
                    dst_ref=arrived.at[d - 1, pl.ds(group * per, per)],
                    send_sem=exchange_sems.at[0, group, d - 1],
                    recv_sem=exchange_sems.at[1, group, d - 1],
                    device_id=(w, at_narrow(d)),
                    device_id_type=MESH,
                )
                copy.start()
                exchanges[group, d] = copy

    half = depth // 2
    crossings, lined, gathers, forwards = {}, {}, {}, {}

    def multiply(ky, carry):
        lefts, rights = [], []
        for d in range(narrow):
            block = sending[n * mine + ky] if d == 0 else arrived[d - 1, ky]
            lefts.append(block.T[:rank_in])
            top, bottom = block[:half, rank_in:], block[half:, rank_in:]
            rights.append(jnp.concatenate([top, bottom], axis=1))
            rights.append(jnp.concatenate([bottom, -top], axis=1))
        left = jnp.concatenate(lefts, axis=1)
        right_high, right_low = split(jnp.concatenate(rights, axis=0))
        for r in range(ranks):
            high, low = split(left * modes[r : r + 1, :])
            lhs_high[r * rank_in : (r + 1) * rank_in] = high
            lhs_low[r * rank_in : (r + 1) * rank_in] = low
        both = jnp.concatenate([right_high, right_low], axis=1)
        width = right_high.shape[1]
        wider = jnp.dot(lhs_high[...], both, preferred_element_type=f32)
        total = jnp.dot(lhs_low[...], right_high, preferred_element_type=f32)
        total += wider[:, :width] + wider[:, width:]
        for r in range(ranks):
            for owner in range(wide):
                at = r * rank_in + owner * share
                part[owner // 2, owner % 2, ky, r * share : (r + 1) * share] = total[at : at + share]
        return carry

    def stage_multiply(group):
        for d in range(1, narrow):
            exchanges[group, d].wait_recv()
        lax.fori_loop(group * per, (group + 1) * per, multiply, 0)
        for l in range(lines):
            copy = pltpu.make_async_remote_copy(
                src_ref=part.at[l, 1 - side, pl.ds(group * per, per)],
                dst_ref=x_arrived.at[l, pl.ds(group * per, per)],
                send_sem=cross_sems.at[0, group, l],
                recv_sem=cross_sems.at[1, group, l],
                device_id=(peer, n),
                device_id_type=MESH,
            )
            copy.start()
            crossings[group, l] = copy

    def stage_cross(group):
        at = pl.ds(group * per, per)
        for l in range(lines):
            crossings[group, l].wait_recv()
        for d in list(range(1, lines)) + [0]:
            to = (line + d) % lines
            z_sending[d, at] = x_arrived[to, at] + part[to, side, at]
            if d:
                copy = pltpu.make_async_remote_copy(
                    src_ref=z_sending.at[d, at],
                    dst_ref=z_arrived.at[d - 1, at],
                    send_sem=line_sems.at[0, group, d - 1],
                    recv_sem=line_sems.at[1, group, d - 1],
                    device_id=(at_line(d), n),
                    device_id_type=MESH,
                )
                copy.start()
                lined[group, d] = copy

    first_scale = 1.0 / (1.0 - 0.9**STEP)
    second_scale = 1.0 / (1.0 - 0.999**STEP)

    def send_steps(owner, group, device, send_sem, recv_sem):
        block = steps_ref.at[owner, pl.ds(group * per, per)]
        copy = pltpu.make_async_remote_copy(
            src_ref=block,
            dst_ref=block,
            send_sem=send_sem,
            recv_sem=recv_sem,
            device_id=(device, n),
            device_id_type=MESH,
        )
        copy.start()
        return copy

    def stage_adam(group):
        at = pl.ds(group * per, per)
        grad = z_sending[0, at]
        for d in range(1, lines):
            lined[group, d].wait_recv()
            grad += z_arrived[d - 1, at]
        new_first = 0.9 * first_ref[at] + 0.1 * grad
        square = grad * grad
        flat = square.reshape(-1, square.shape[-1])
        other = pltpu.roll(flat, flat.shape[-1] // 2, 1).reshape(square.shape)
        new_second = 0.999 * second_ref[at] + 0.001 * (square + other)
        first_out[at] = new_first
        second_out[at] = new_second
        steps_ref[w, at] = new_first * first_scale / (jnp.sqrt(new_second * second_scale) + 1e-08)
        forwards[group, 0] = send_steps(
            w, group, peer, forward_sems.at[0, group, 0], forward_sems.at[1, group, 0]
        )
        for d in range(1, lines):
            gathers[group, d] = send_steps(
                w, group, at_line(d), gather_sems.at[0, group, d - 1], gather_sems.at[1, group, d - 1]
            )

    def stage_forward(group):
        for d in range(1, lines):
            gathers[group, d].wait_recv()
            forwards[group, d] = send_steps(
                at_line(lines - d), group, peer, forward_sems.at[0, group, d], forward_sems.at[1, group, d]
            )

    for tick in range(groups + 3):
        for late, stage in enumerate((stage_multiply, stage_cross, stage_adam, stage_forward)):
            if 0 <= tick - late < groups:
                stage(tick - late)
    for copy in forwards.values():
        copy.wait_recv()
    for copies in (exchanges, crossings, lined, gathers, forwards):
        for copy in copies.values():
            copy.wait_send()


def update_kernel(
    mode_ref, steps_ref, weights_ref, out_ref, in_ref, result_ref, out_pair, in_stack
):
    ky, tile = pl.program_id(0), pl.program_id(1)
    rows = weights_ref.shape[1]
    ranks = steps_ref.shape[1]
    rank_in = steps_ref.shape[2]
    columns = weights_ref.shape[4]
    start = (lax.axis_index("wide") * pl.num_programs(1) + tile) * rows

    @pl.when((ky == 0) & (tile == 0))
    def prepare():
        clear = jnp.zeros(out_ref.shape, f32)
        flat = out_ref[...]
        pair = jnp.concatenate(
            [jnp.concatenate([flat, clear], axis=1), jnp.concatenate([clear, flat], axis=1)], axis=0
        )
        high, low = split(pair)
        out_pair[0] = high
        out_pair[1] = low
        scaled = 0.3 * in_ref[...]
        rounded = scaled.astype(bf16).astype(f32)
        stack = jnp.concatenate([rounded, rounded, scaled - rounded], axis=0)
        in_stack[...] = stack.T.astype(bf16)

    expanded = []
    for x in range(rows):
        total = mode_ref[0, start + x] * steps_ref[0, 0]
        for r in range(1, ranks):
            total += mode_ref[r, start + x] * steps_ref[0, r]
        expanded.append(total)
    high, low = split(jnp.concatenate(expanded, axis=0))
    left = jnp.dot(high, out_pair[0], preferred_element_type=f32)
    left += jnp.dot(low, out_pair[0], preferred_element_type=f32)
    left += jnp.dot(high, out_pair[1], preferred_element_type=f32)
    for x in range(rows):
        high, low = split(left[x * rank_in : (x + 1) * rank_in])
        change = jnp.dot(
            in_stack[...], jnp.concatenate([high, low, high], axis=0), preferred_element_type=f32
        )
        for p in range(2):
            result_ref[p, x, 0] = weights_ref[p, x, 0] - change[:, p * columns : (p + 1) * columns]


def local(
    spectra, out_grads, weights, mode_factor, in_factor, out_factor, first_moment, second_moment
):
    wide = lax.axis_size("wide")
    narrow = lax.axis_size("narrow")
    samples = spectra.shape[1]
    assert samples == 1
    modes_first, modes_second, channels = spectra.shape[2:]
    first_mine = modes_first // wide
    second_mine = modes_second // narrow
    rank_in = in_factor.shape[1]
    rank_out = out_factor.shape[1]
    ranks = mode_factor.shape[1]
    share = rank_in // wide
    width = 2 * rank_out
    depth = 2 * modes_first
    lines = wide // 2
    groups = 4
    shard_rows = ranks * share

    first = first_moment.reshape(2, ranks, second_mine, share, rank_out)
    first = first.transpose(2, 1, 3, 0, 4).reshape(second_mine, shard_rows, width)
    second = second_moment.reshape(ranks, second_mine, share, 1, rank_out)
    second = jnp.broadcast_to(second, (ranks, second_mine, share, 2, rank_out))
    second = second.transpose(1, 0, 2, 3, 4).reshape(second_mine, shard_rows, width)

    vmem = pl.BlockSpec(memory_space=pltpu.VMEM)
    steps, new_first, new_second = pl.pallas_call(
        functools.partial(exchange_kernel, wide, narrow, groups),
        out_shape=(
            jax.ShapeDtypeStruct((wide, second_mine, shard_rows, width), f32),
            jax.ShapeDtypeStruct((second_mine, shard_rows, width), f32),
            jax.ShapeDtypeStruct((second_mine, shard_rows, width), f32),
        ),
        in_specs=[vmem] * 7,
        out_specs=(vmem,) * 3,
        scratch_shapes=[
            pltpu.VMEM((depth * modes_second, width), f32),
            pltpu.VMEM((modes_second, depth, width), f32),
            pltpu.VMEM((narrow - 1, second_mine, depth, width), f32),
            pltpu.VMEM((ranks * rank_in, narrow * depth), bf16),
            pltpu.VMEM((ranks * rank_in, narrow * depth), bf16),
            pltpu.VMEM((lines, 2, second_mine, shard_rows, width), f32),
            pltpu.VMEM((lines, second_mine, shard_rows, width), f32),
            pltpu.VMEM((lines, second_mine, shard_rows, width), f32),
            pltpu.VMEM((lines - 1, second_mine, shard_rows, width), f32),
            pltpu.SemaphoreType.DMA((2, groups, narrow - 1)),
            pltpu.SemaphoreType.DMA((2, groups, lines)),
            pltpu.SemaphoreType.DMA((2, groups, lines - 1)),
            pltpu.SemaphoreType.DMA((2, groups, lines - 1)),
            pltpu.SemaphoreType.DMA((2, groups, lines)),
        ],
        compiler_params=pltpu.CompilerParams(
            collective_id=0, has_side_effects=True, vmem_limit_bytes=48 * 1024 * 1024
        ),
        name="core_exchange",
    )(
        spectra.reshape(depth * modes_second, channels),
        out_grads.reshape(depth * modes_second, channels),
        in_factor.T,
        out_factor.T,
        mode_factor.T,
        first,
        second,
    )

    steps = steps.reshape(wide, second_mine, ranks, share, width)
    steps = steps.transpose(1, 2, 0, 3, 4).reshape(second_mine, ranks, rank_in, width)

    rows = min(4, first_mine)
    block = pl.BlockSpec(
        (2, rows, 1, channels, channels), lambda ky, tile: (0, tile, ky, 0, 0)
    )
    new_weights = pl.pallas_call(
        update_kernel,
        grid=(second_mine, first_mine // rows),
        out_shape=jax.ShapeDtypeStruct(weights.shape, f32),
        in_specs=[
            pl.BlockSpec(memory_space=pltpu.SMEM),
            pl.BlockSpec((1, ranks, rank_in, width), lambda ky, tile: (ky, 0, 0, 0)),
            block,
            pl.BlockSpec((rank_out, channels), lambda ky, tile: (0, 0)),
            pl.BlockSpec((rank_in, channels), lambda ky, tile: (0, 0)),
        ],
        out_specs=block,
        scratch_shapes=[
            pltpu.VMEM((2, width, 2 * channels), bf16),
            pltpu.VMEM((channels, 3 * rank_in), bf16),
        ],
        compiler_params=pltpu.CompilerParams(vmem_limit_bytes=48 * 1024 * 1024),
        name="weight_update",
    )(mode_factor.T, steps, weights, out_factor.T, in_factor.T)

    new_first = new_first.reshape(second_mine, ranks, share, 2, rank_out)
    new_first = new_first.transpose(3, 1, 0, 2, 4).reshape(first_moment.shape)
    new_second = new_second[:, :, :rank_out].reshape(second_mine, ranks, share, rank_out)
    new_second = new_second.transpose(1, 0, 2, 3).reshape(second_moment.shape)
    return (new_weights, new_first, new_second)


def solution(mesh):
    placed = (
        P(None, ("wide", "narrow"), None, None, None),
        P(None, ("wide", "narrow"), None, None, None),
        P(None, "wide", "narrow", None, None),
        P(),
        P(),
        P(),
        P(None, None, "narrow", "wide"),
        P(None, "narrow", "wide"),
    )
    return jax.shard_map(
        local,
        mesh=mesh,
        in_specs=placed,
        out_specs=(
            P(None, "wide", "narrow", None, None),
            P(None, None, "narrow", "wide"),
            P(None, "narrow", "wide"),
        ),
        check_vma=False,
    )
```

```python
import functools

import jax
import jax.numpy as jnp
from jax import lax
from jax.experimental import pallas as pl
from jax.experimental.pallas import tpu as pltpu
from jax.sharding import PartitionSpec as P

STEP = 1000
MESH = pl.DeviceIdType.MESH
f32 = jnp.float32
bf16 = jnp.bfloat16


def split(value):
    high = value.astype(bf16)
    return high, (value - high.astype(f32)).astype(bf16)


def exchange_kernel(
    wide,
    narrow,
    groups,
    x_ref,
    g_ref,
    in_ref,
    out_ref,
    mode_ref,
    first_ref,
    second_ref,
    steps_ref,
    first_out,
    second_out,
    projected,
    sending,
    arrived,
    lhs_high,
    lhs_low,
    part,
    x_arrived,
    z_sending,
    z_arrived,
    exchange_sems,
    cross_sems,
    line_sems,
    gather_sems,
    forward_sems,
):
    lines = wide // 2
    w = lax.axis_index("wide")
    n = lax.axis_index("narrow")
    line = w // 2
    side = w % 2
    peer = line * 2 + (1 - side)
    ranks = mode_ref.shape[0]
    depth = arrived.shape[2]
    mine = arrived.shape[1]
    per = mine // groups
    rank_in = projected.shape[1] // 2
    share = rank_in // wide
    stride = sending.shape[0]

    def at_line(d):
        return ((line + d) % lines) * 2 + side

    def at_narrow(d):
        return (n + d) % narrow

    barrier = pltpu.get_barrier_semaphore()
    for d in range(1, narrow):
        pl.semaphore_signal(barrier, inc=1, device_id=(w, at_narrow(d)), device_id_type=MESH)
    for d in range(1, lines):
        pl.semaphore_signal(barrier, inc=1, device_id=(at_line(d), n), device_id_type=MESH)
    pl.semaphore_signal(barrier, inc=1, device_id=(peer, n), device_id_type=MESH)
    rows = 512
    modes = jnp.concatenate([mode_ref[...]] * (2 * narrow), axis=1)
    none = jnp.zeros(in_ref.shape, f32)
    x_high, x_low = split(jnp.concatenate([in_ref[...], none], axis=0).T)
    g_high, g_low = split(jnp.concatenate([none, out_ref[...]], axis=0).T)

    def project(index, carry):
        at = pl.ds(pl.multiple_of(index * rows, rows), rows)
        xs, gs = x_ref[at, :], g_ref[at, :]
        total = jnp.dot(xs, x_high, preferred_element_type=f32)
        total += jnp.dot(gs, g_high, preferred_element_type=f32)
        total += jnp.dot(xs, x_low, preferred_element_type=f32)
        total += jnp.dot(gs, g_low, preferred_element_type=f32)
        projected[at, :] = total
        return carry

    lax.fori_loop(0, x_ref.shape[0] // rows, project, 0)

    def collect(ky):
        sending[ky] = projected[pl.ds(ky, depth, stride=stride), :]

    pl.semaphore_wait(barrier, narrow - 1 + lines - 1 + 1)
    exchanges = {}
    for group in range(groups):
        for d in list(range(1, narrow)) + [0]:
            start = at_narrow(d) * mine + group * per

            def one(index, carry):
                collect(start + index)
                return carry

            lax.fori_loop(0, per, one, 0)
            if d:
                copy = pltpu.make_async_remote_copy(
                    src_ref=sending.at[pl.ds(start, per)],
                    dst_ref=arrived.at[d - 1, pl.ds(group * per, per)],
                    send_sem=exchange_sems.at[0, group, d - 1],
                    recv_sem=exchange_sems.at[1, group, d - 1],
                    device_id=(w, at_narrow(d)),
                    device_id_type=MESH,
                )
                copy.start()
                exchanges[group, d] = copy

    half = depth // 2
    crossings, lined, gathers, forwards = {}, {}, {}, {}

    def multiply(ky, carry):
        lefts, rights = [], []
        for d in range(narrow):
            block = sending[n * mine + ky] if d == 0 else arrived[d - 1, ky]
            lefts.append(block.T[:rank_in])
            top, bottom = block[:half, rank_in:], block[half:, rank_in:]
            rights.append(jnp.concatenate([top, bottom], axis=1))
            rights.append(jnp.concatenate([bottom, -top], axis=1))
        left = jnp.concatenate(lefts, axis=1)
        right_high, right_low = split(jnp.concatenate(rights, axis=0))
        for r in range(ranks):
            high, low = split(left * modes[r : r + 1, :])
            lhs_high[r * rank_in : (r + 1) * rank_in] = high
            lhs_low[r * rank_in : (r + 1) * rank_in] = low
        both = jnp.concatenate([right_high, right_low], axis=1)
        width = right_high.shape[1]
        wider = jnp.dot(lhs_high[...], both, preferred_element_type=f32)
        total = jnp.dot(lhs_low[...], right_high, preferred_element_type=f32)
        total += wider[:, :width] + wider[:, width:]
        for r in range(ranks):
            for owner in range(wide):
                at = r * rank_in + owner * share
                part[owner // 2, owner % 2, ky, r * share : (r + 1) * share] = total[at : at + share]
        return carry

    def stage_multiply(group):
        for d in range(1, narrow):
            exchanges[group, d].wait_recv()
        lax.fori_loop(group * per, (group + 1) * per, multiply, 0)
        for l in range(lines):
            copy = pltpu.make_async_remote_copy(
                src_ref=part.at[l, 1 - side, pl.ds(group * per, per)],
                dst_ref=x_arrived.at[l, pl.ds(group * per, per)],
                send_sem=cross_sems.at[0, group, l],
                recv_sem=cross_sems.at[1, group, l],
                device_id=(peer, n),
                device_id_type=MESH,
            )
            copy.start()
            crossings[group, l] = copy

    def stage_cross(group):
        at = pl.ds(group * per, per)
        for l in range(lines):
            crossings[group, l].wait_recv()
        for d in list(range(1, lines)) + [0]:
            to = (line + d) % lines
            z_sending[d, at] = x_arrived[to, at] + part[to, side, at]
            if d:
                copy = pltpu.make_async_remote_copy(
                    src_ref=z_sending.at[d, at],
                    dst_ref=z_arrived.at[d - 1, at],
                    send_sem=line_sems.at[0, group, d - 1],
                    recv_sem=line_sems.at[1, group, d - 1],
                    device_id=(at_line(d), n),
                    device_id_type=MESH,
                )
                copy.start()
                lined[group, d] = copy

    first_scale = 1.0 / (1.0 - 0.9**STEP)
    second_scale = 1.0 / (1.0 - 0.999**STEP)

    def send_steps(owner, group, device, send_sem, recv_sem):
        block = steps_ref.at[owner, pl.ds(group * per, per)]
        copy = pltpu.make_async_remote_copy(
            src_ref=block,
            dst_ref=block,
            send_sem=send_sem,
            recv_sem=recv_sem,
            device_id=(device, n),
            device_id_type=MESH,
        )
        copy.start()
        return copy

    def stage_adam(group):
        at = pl.ds(group * per, per)
        grad = z_sending[0, at]
        for d in range(1, lines):
            lined[group, d].wait_recv()
            grad += z_arrived[d - 1, at]
        new_first = 0.9 * first_ref[at] + 0.1 * grad
        square = grad * grad
        flat = square.reshape(-1, square.shape[-1])
        other = pltpu.roll(flat, flat.shape[-1] // 2, 1).reshape(square.shape)
        new_second = 0.999 * second_ref[at] + 0.001 * (square + other)
        first_out[at] = new_first
        second_out[at] = new_second
        steps_ref[w, at] = new_first * first_scale / (jnp.sqrt(new_second * second_scale) + 1e-08)
        forwards[group, 0] = send_steps(
            w, group, peer, forward_sems.at[0, group, 0], forward_sems.at[1, group, 0]
        )
        for d in range(1, lines):
            gathers[group, d] = send_steps(
                w, group, at_line(d), gather_sems.at[0, group, d - 1], gather_sems.at[1, group, d - 1]
            )

    def stage_forward(group):
        for d in range(1, lines):
            gathers[group, d].wait_recv()
            forwards[group, d] = send_steps(
                at_line(lines - d), group, peer, forward_sems.at[0, group, d], forward_sems.at[1, group, d]
            )

    for tick in range(groups + 3):
        for late, stage in enumerate((stage_multiply, stage_cross, stage_adam, stage_forward)):
            if 0 <= tick - late < groups:
                stage(tick - late)
    for copy in forwards.values():
        copy.wait_recv()
    for copies in (exchanges, crossings, lined, gathers, forwards):
        for copy in copies.values():
            copy.wait_send()


def update_kernel(
    mode_ref, steps_ref, weights_ref, out_ref, in_ref, result_ref, out_pair, in_stack
):
    ky, tile = pl.program_id(0), pl.program_id(1)
    rows = weights_ref.shape[1]
    ranks = steps_ref.shape[1]
    rank_in = steps_ref.shape[2]
    columns = weights_ref.shape[4]
    start = (lax.axis_index("wide") * pl.num_programs(1) + tile) * rows

    @pl.when((ky == 0) & (tile == 0))
    def prepare():
        clear = jnp.zeros(out_ref.shape, f32)
        flat = out_ref[...]
        pair = jnp.concatenate(
            [jnp.concatenate([flat, clear], axis=1), jnp.concatenate([clear, flat], axis=1)], axis=0
        )
        high, low = split(pair)
        out_pair[0] = high
        out_pair[1] = low
        scaled = 0.3 * in_ref[...]
        rounded = scaled.astype(bf16).astype(f32)
        stack = jnp.concatenate([rounded, rounded, scaled - rounded], axis=0)
        in_stack[...] = stack.T.astype(bf16)

    expanded = []
    for x in range(rows):
        total = mode_ref[0, start + x] * steps_ref[0, 0]
        for r in range(1, ranks):
            total += mode_ref[r, start + x] * steps_ref[0, r]
        expanded.append(total)
    high, low = split(jnp.concatenate(expanded, axis=0))
    left = jnp.dot(high, out_pair[0], preferred_element_type=f32)
    left += jnp.dot(low, out_pair[0], preferred_element_type=f32)
    left += jnp.dot(high, out_pair[1], preferred_element_type=f32)
    for x in range(rows):
        high, low = split(left[x * rank_in : (x + 1) * rank_in])
        change = jnp.dot(
            in_stack[...], jnp.concatenate([high, low, high], axis=0), preferred_element_type=f32
        )
        for p in range(2):
            result_ref[p, x, 0] = weights_ref[p, x, 0] - change[:, p * columns : (p + 1) * columns]


def local(
    spectra, out_grads, weights, mode_factor, in_factor, out_factor, first_moment, second_moment
):
    wide = lax.axis_size("wide")
    narrow = lax.axis_size("narrow")
    samples = spectra.shape[1]
    assert samples == 1
    modes_first, modes_second, channels = spectra.shape[2:]
    first_mine = modes_first // wide
    second_mine = modes_second // narrow
    rank_in = in_factor.shape[1]
    rank_out = out_factor.shape[1]
    ranks = mode_factor.shape[1]
    share = rank_in // wide
    width = 2 * rank_out
    depth = 2 * modes_first
    lines = wide // 2
    groups = second_mine
    shard_rows = ranks * share

    first = first_moment.reshape(2, ranks, second_mine, share, rank_out)
    first = first.transpose(2, 1, 3, 0, 4).reshape(second_mine, shard_rows, width)
    second = second_moment.reshape(ranks, second_mine, share, 1, rank_out)
    second = jnp.broadcast_to(second, (ranks, second_mine, share, 2, rank_out))
    second = second.transpose(1, 0, 2, 3, 4).reshape(second_mine, shard_rows, width)

    vmem = pl.BlockSpec(memory_space=pltpu.VMEM)
    steps, new_first, new_second = pl.pallas_call(
        functools.partial(exchange_kernel, wide, narrow, groups),
        out_shape=(
            jax.ShapeDtypeStruct((wide, second_mine, shard_rows, width), f32),
            jax.ShapeDtypeStruct((second_mine, shard_rows, width), f32),
            jax.ShapeDtypeStruct((second_mine, shard_rows, width), f32),
        ),
        in_specs=[vmem] * 7,
        out_specs=(vmem,) * 3,
        scratch_shapes=[
            pltpu.VMEM((depth * modes_second, width), f32),
            pltpu.VMEM((modes_second, depth, width), f32),
            pltpu.VMEM((narrow - 1, second_mine, depth, width), f32),
            pltpu.VMEM((ranks * rank_in, narrow * depth), bf16),
            pltpu.VMEM((ranks * rank_in, narrow * depth), bf16),
            pltpu.VMEM((lines, 2, second_mine, shard_rows, width), f32),
            pltpu.VMEM((lines, second_mine, shard_rows, width), f32),
            pltpu.VMEM((lines, second_mine, shard_rows, width), f32),
            pltpu.VMEM((lines - 1, second_mine, shard_rows, width), f32),
            pltpu.SemaphoreType.DMA((2, groups, narrow - 1)),
            pltpu.SemaphoreType.DMA((2, groups, lines)),
            pltpu.SemaphoreType.DMA((2, groups, lines - 1)),
            pltpu.SemaphoreType.DMA((2, groups, lines - 1)),
            pltpu.SemaphoreType.DMA((2, groups, lines)),
        ],
        compiler_params=pltpu.CompilerParams(
            collective_id=0, has_side_effects=True, vmem_limit_bytes=48 * 1024 * 1024
        ),
        name="core_exchange",
    )(
        spectra.reshape(depth * modes_second, channels),
        out_grads.reshape(depth * modes_second, channels),
        in_factor.T,
        out_factor.T,
        mode_factor.T,
        first,
        second,
    )

    steps = steps.reshape(wide, second_mine, ranks, share, width)
    steps = steps.transpose(1, 2, 0, 3, 4).reshape(second_mine, ranks, rank_in, width)

    rows = min(4, first_mine)
    block = pl.BlockSpec(
        (2, rows, 1, channels, channels), lambda ky, tile: (0, tile, ky, 0, 0)
    )
    new_weights = pl.pallas_call(
        update_kernel,
        grid=(second_mine, first_mine // rows),
        out_shape=jax.ShapeDtypeStruct(weights.shape, f32),
        in_specs=[
            pl.BlockSpec(memory_space=pltpu.SMEM),
            pl.BlockSpec((1, ranks, rank_in, width), lambda ky, tile: (ky, 0, 0, 0)),
            block,
            pl.BlockSpec((rank_out, channels), lambda ky, tile: (0, 0)),
            pl.BlockSpec((rank_in, channels), lambda ky, tile: (0, 0)),
        ],
        out_specs=block,
        scratch_shapes=[
            pltpu.VMEM((2, width, 2 * channels), bf16),
            pltpu.VMEM((channels, 3 * rank_in), bf16),
        ],
        compiler_params=pltpu.CompilerParams(vmem_limit_bytes=48 * 1024 * 1024),
        name="weight_update",
    )(mode_factor.T, steps, weights, out_factor.T, in_factor.T)

    new_first = new_first.reshape(second_mine, ranks, share, 2, rank_out)
    new_first = new_first.transpose(3, 1, 0, 2, 4).reshape(first_moment.shape)
    new_second = new_second[:, :, :rank_out].reshape(second_mine, ranks, share, rank_out)
    new_second = new_second.transpose(1, 0, 2, 3).reshape(second_moment.shape)
    return (new_weights, new_first, new_second)


def solution(mesh):
    placed = (
        P(None, ("wide", "narrow"), None, None, None),
        P(None, ("wide", "narrow"), None, None, None),
        P(None, "wide", "narrow", None, None),
        P(),
        P(),
        P(),
        P(None, None, "narrow", "wide"),
        P(None, "narrow", "wide"),
    )
    return jax.shard_map(
        local,
        mesh=mesh,
        in_specs=placed,
        out_specs=(
            P(None, "wide", "narrow", None, None),
            P(None, None, "narrow", "wide"),
            P(None, "narrow", "wide"),
        ),
        check_vma=False,
    )
```
